256 devices in a mesh: member: 16 (over z, core), basin: 16 (over y, x).
Axes of the slice: x: 4, y: 4, z: 8, core: 2. Of those that a mesh axis runs over, the one named last changes fastest.
Arguments:
- prior_params: float32 [512, 8, 2048], P('member', None, 'basin'), may hold values from -3 to 3
- lateral_flow: float32 [512, 2, 262144], P('member', None, 'basin'), may hold values from 0.2 to 2
- inflow_start: float32 [262144], P('basin'), may hold values from 0.5 to 4
- outflow_start: float32 [262144], P('basin'), may hold values from 0.5 to 4
- reach_count: int32 [2048], P('basin'), may hold values from 64 to 128
- downstream: int32 [2048], P('basin'), may hold values from 0 to 63
- gauge_reach: int32 [8192], P('basin'), may hold values from 0 to 16383
- observed: float32 [2, 8192], P(None, 'basin'), may hold values from 0.5 to 4
- obs_var: float32 [2, 8192], P(None, 'basin'), may hold values from 0.02 to 0.5
- obs_noise: float32 [512, 2, 8192], P('member', None, 'basin'), may hold values from -4 to 4
Outputs:
- posterior: float32 [512, 8, 2048], P('member', None, 'basin')
- predicted: float32 [512, 2, 8192], P('member', None, 'basin')
The draws below stay inside these ranges and needn't reach their ends.
All inputs are finite; a program needn't handle non-finite values.
Results may differ from the reference program's by a relative error of at most 0.0003.
Values sent between devices are 32-bit elements; how exact they have to be, the bound alone decides.
No kernel may reach another device: no remote copies, remote signals or barrier semaphores. Data moves between devices by JAX's collectives and lax.ppermute only.
A program may use at most 128 MiB of HBM per device.

```python
import math
import jax
import jax.numpy as jnp
from jax import lax

LANES = 128
NPAR = 8
HOURS = 2
M_DEV = 32
BLK_LEV = 64
LEV_DEV = 2
GAUGE_DEV = 512
MEMBERS = 512
LEVELS = 32
BLOCKS = 2048
REACHES = 262144
GAUGES = 8192
N_MEMBER = 16


def draw_reach_count(key, part):
    counts = jax.random.randint(key, (BLOCKS,), 64, 129, dtype=jnp.int32)
    return counts.at[0].set(128)


def with_ends(array, key, low, high):
    spot = [jax.random.randint(jax.random.fold_in(key, axis), (), 0, length) for axis, length in enumerate(array.shape)]
    longest = array.shape.index(max(array.shape))
    neighbour = spot[:longest] + [(spot[longest] + 1) % array.shape[longest]] + spot[longest + 1:]
    return array.at[tuple(spot)].set(low).at[tuple(neighbour)].set(high)


def level_of(stream_key, shape, split, least, top_value):
    loudness = 1.0
    for dim, shards_of in split:
        draws = jax.random.uniform(jax.random.fold_in(jax.random.fold_in(stream_key, 6), dim), (shards_of,), jnp.float32, least / len(split), top_value / len(split))
        loudness = loudness * jnp.repeat(jnp.exp(draws), shape[dim] // shards_of).reshape((-1,) + (1,) * (len(shape) - 1 - dim))
    return loudness


def scatter_about(key, shape, deviation, most, shards=(), kind=jnp.bfloat16):
    loudness = level_of(key, shape, shards, -0.22, 0.18) if shards else 1.0
    entries = jax.random.normal(key, shape, jnp.float32) * deviation * loudness
    return jnp.minimum(jnp.maximum(entries, -most), most).astype(kind)


def setup_inputs(seed: int = 0) -> dict:
    seeds = jax.random.split(jax.random.key(seed), 11)
    prior_params = scatter_about(seeds[0], (MEMBERS, NPAR, BLOCKS), 0.7, 3.0, ((0, 16), (2, 16)), jnp.float32)
    lateral_flow = jnp.clip(jnp.exp(math.log(2.0) - 2.3025851 * jax.random.uniform(seeds[1], (MEMBERS, HOURS, REACHES), jnp.float32) ** level_of(seeds[1], (MEMBERS, HOURS, REACHES), ((0, 16), (2, 16)), -0.2, 0.2)), 0.2, 2.0)
    inflow_start = jnp.clip(0.5 + 3.5 * jax.random.uniform(seeds[2], (REACHES,), jnp.float32) ** level_of(seeds[2], (REACHES,), ((0, 16),), -0.2, 0.2), 0.5, 4.0)
    outflow_start = jnp.clip(0.5 + 3.5 * jax.random.uniform(seeds[3], (REACHES,), jnp.float32) ** level_of(seeds[3], (REACHES,), ((0, 16),), -0.2, 0.2), 0.5, 4.0)
    reach_count = draw_reach_count(jax.random.fold_in(seeds[10], 71), 0)
    downstream = with_ends(jax.random.randint(seeds[5], (BLOCKS,), 0, BLK_LEV), jax.random.fold_in(seeds[5], 1), 0, BLK_LEV - 1).astype(jnp.int32)
    gauge_reach = with_ends(jax.random.randint(seeds[6], (GAUGES,), 0, BLK_LEV * LEV_DEV * LANES), jax.random.fold_in(seeds[6], 1), 0, (BLK_LEV * LEV_DEV * LANES) - 1).astype(jnp.int32)
    observed = jnp.clip(0.5 + 3.5 * jax.random.uniform(seeds[7], (HOURS, GAUGES), jnp.float32) ** level_of(seeds[7], (HOURS, GAUGES), ((1, 16),), -0.2, 0.2), 0.5, 4.0)
    obs_var = jnp.clip(jnp.exp(math.log(0.5) - 3.218876 * jax.random.uniform(seeds[8], (HOURS, GAUGES), jnp.float32) ** level_of(seeds[8], (HOURS, GAUGES), ((1, 16),), -0.2, 0.2)), 0.02, 0.5)
    obs_noise = scatter_about(seeds[9], (MEMBERS, HOURS, GAUGES), 1.0, 4.0, ((0, 16), (2, 16)), jnp.float32)
    return dict(prior_params=prior_params, lateral_flow=lateral_flow, inflow_start=inflow_start, outflow_start=outflow_start, reach_count=reach_count, downstream=downstream, gauge_reach=gauge_reach, observed=observed, obs_var=obs_var, obs_noise=obs_noise)


exact_mode = lax.Precision.HIGHEST

def inverse_sinh(values):
    return jnp.log(values + jnp.sqrt(values * values + 1.0))

def route_coefficients(prior_params):
    storage = 0.02 + 0.1 * jax.nn.sigmoid(prior_params[:, 0, :])
    weighting = 0.2 * jax.nn.sigmoid(prior_params[:, 1, :])
    denominator = storage * (1.0 - weighting) + 0.5
    weight_now = (0.5 - storage * weighting) / denominator
    weight_back = (0.5 + storage * weighting) / denominator
    weight_carry = (storage * (1.0 - weighting) - 0.5) / denominator
    return (weight_now[:, :, None], weight_back[:, :, None], weight_carry[:, :, None])

def lateral_scaling(prior_params, lane_count):
    lane_pos = jnp.arange(lane_count, dtype=jnp.float32)
    orders = jnp.arange(6, dtype=jnp.float32)
    cosine_modes = jnp.cos(math.pi * orders[:, None] * (lane_pos[None, :] + 0.5) / lane_count)
    exponent = jnp.einsum('mkb,kr->mbr', 0.2 * prior_params[:, 2:, :], cosine_modes, precision=exact_mode)
    return jnp.exp(exponent)

def solve_gram(gram_matrix, cross_matrix):
    factor = jnp.linalg.cholesky(gram_matrix)
    halfway = lax.linalg.triangular_solve(factor, cross_matrix, left_side=True, lower=True)
    return lax.linalg.triangular_solve(factor, halfway, left_side=True, lower=True, transpose_a=True)

def to_levels(values, group_size):
    shaped = values.reshape((group_size, LEVELS, BLK_LEV) + values.shape[2:])
    return jnp.moveaxis(shaped, 1, 0)

def reference(prior_params, lateral_flow, inflow_start, outflow_start, reach_count, downstream, gauge_reach, observed, obs_var, obs_noise):
    lane_ids = jnp.arange(LANES, dtype=jnp.int32)
    live_mask = (lane_ids[None, :] < reach_count[:, None]).astype(jnp.float32).reshape(LEVELS, BLK_LEV, LANES)
    targets = jnp.arange(BLK_LEV, dtype=jnp.int32)
    one_hot = (downstream.reshape(LEVELS, BLK_LEV)[:, None, :] == targets[None, :, None]).astype(jnp.float32)
    start_in = inflow_start.reshape(LEVELS, BLK_LEV, LANES) * live_mask
    start_out = outflow_start.reshape(LEVELS, BLK_LEV, LANES) * live_mask
    flat_index = jnp.arange(GAUGES, dtype=jnp.int32) // GAUGE_DEV * (BLK_LEV * LEV_DEV * LANES) + gauge_reach

    def one_group(operands):
        prior_group, lateral_group = operands
        group_size = prior_group.shape[0]
        weight_now, weight_back, weight_carry = route_coefficients(prior_group)
        scaling = lateral_scaling(prior_group, LANES)
        now_lev = to_levels(weight_now, group_size)
        back_lev = to_levels(weight_back, group_size)
        carry_lev = to_levels(weight_carry, group_size)
        scale_lev = to_levels(scaling, group_size)
        prev_in = jnp.broadcast_to(start_in[:, None], (LEVELS, group_size, BLK_LEV, LANES))
        prev_out = jnp.broadcast_to(start_out[:, None], (LEVELS, group_size, BLK_LEV, LANES))
        results = []
        for hour_idx in range(HOURS):
            lateral_lev = to_levels(lateral_group[:, hour_idx].reshape(group_size, BLOCKS, LANES), group_size)

            def level_step(upstream, pieces):
                coef_now, coef_back, coef_carry, scale_now, lateral_now, mask_now, hot_now, old_in, old_out = pieces
                inflow = mask_now * (lateral_now * scale_now + upstream)
                outflow = coef_now * inflow + coef_back * old_in + coef_carry * old_out
                downstream_in = jnp.einsum('nj,gjr->gnr', hot_now, outflow, precision=exact_mode)
                return (downstream_in, (inflow, outflow))
            initial = jnp.zeros((group_size, BLK_LEV, LANES), jnp.float32)
            _, (prev_in, prev_out) = lax.scan(level_step, initial, (now_lev, back_lev, carry_lev, scale_lev, lateral_lev, live_mask, one_hot, prev_in, prev_out))
            flat = jnp.moveaxis(prev_out, 0, 1).reshape(group_size, REACHES)
            results.append(inverse_sinh(flat[:, flat_index]))
        return jnp.stack(results, 1)
    grouped = lax.map(one_group, (prior_params.reshape(N_MEMBER, M_DEV, NPAR, BLOCKS), lateral_flow.reshape(N_MEMBER, M_DEV, HOURS, REACHES)))
    predicted = grouped.reshape(MEMBERS, HOURS, GAUGES)
    spread = jnp.sqrt(obs_var)
    spread_root = math.sqrt(MEMBERS - 1.0)
    mean_pred = lax.optimization_barrier(jnp.sum(predicted, 0)) / MEMBERS
    scaled = (predicted - mean_pred) / (spread_root * (2.0 * spread))
    innovation = (observed + 2.0 * spread * obs_noise - predicted) / (2.0 * spread)
    scaled_rows = scaled.reshape(MEMBERS, HOURS * GAUGES)
    innov_rows = innovation.reshape(MEMBERS, HOURS * GAUGES)
    gram_matrix = jnp.dot(scaled_rows.astype(jnp.float32), scaled_rows.T.astype(jnp.float32), precision=exact_mode, preferred_element_type=jnp.float32)
    cross_matrix = jnp.dot(scaled_rows.astype(jnp.float32), innov_rows.T.astype(jnp.float32), precision=exact_mode, preferred_element_type=jnp.float32)
    gram_matrix = gram_matrix + jnp.eye(MEMBERS, dtype=jnp.float32)
    solved = solve_gram(gram_matrix, cross_matrix)
    mean_prior = lax.optimization_barrier(jnp.sum(prior_params, 0)) / MEMBERS
    anomaly = (prior_params - mean_prior) / spread_root
    posterior = prior_params + jnp.einsum('mn,mkb->nkb', solved, anomaly, precision=exact_mode)
    return (posterior, predicted)
```

```python
import math

import jax
import jax.numpy as jnp
import numpy as np
from jax import lax
from jax.experimental import pallas as pl
from jax.experimental.pallas import tpu as pltpu
from jax.sharding import PartitionSpec as P

LANES = 128
BLK_LEV = 64
GROUP = 8
FLOW_ROWS = 256
SEND_ROWS = 272

exact_mode = lax.Precision.HIGHEST


def inverse_sinh(values):
    return jnp.log(values + jnp.sqrt(values * values + 1.0))


def two_terms(values):
    high = values.astype(jnp.bfloat16)
    low = (values - high.astype(jnp.float32)).astype(jnp.bfloat16)
    return jnp.concatenate([high, low], axis=0)


def drain_matrix(target_row):
    rows = lax.broadcasted_iota(jnp.int32, (BLK_LEV, LANES), 0).astype(jnp.float32)
    return jnp.where(rows == target_row, 1.0, 0.0).astype(jnp.bfloat16)


def drain(matrix, flows):
    return jnp.dot(matrix, two_terms(flows), preferred_element_type=jnp.float32)


def column(matrix, index):
    return jnp.broadcast_to(matrix[:, index : index + 1], (matrix.shape[0], LANES))


def gauge_places(meta):
    slots = meta[3:7, :].astype(jnp.int32)
    return slots >> 7, slots & 127


def read_gauges(flows, block_rows, lane_rows):
    rows = lax.broadcasted_iota(jnp.int32, flows.shape, 0)
    read = []
    for group in range(4):
        lanes = jnp.broadcast_to(lane_rows[group : group + 1, :], flows.shape)
        picked = jnp.take_along_axis(flows, lanes, axis=1, mode="promise_in_bounds")
        mine = rows == block_rows[group : group + 1, :]
        read.append(jnp.sum(jnp.where(mine, picked, 0.0), axis=0, keepdims=True))
    return jnp.concatenate(read, axis=0)


def local_kernel(prior_ref, lateral_ref, in_ref, out_ref, meta_ref, modes_ref, send_ref, local_ref):
    meta = meta_ref[...]
    storage = 0.02 + 0.1 * jax.nn.sigmoid(prior_ref[:, 0, :])
    weighting = 0.2 * jax.nn.sigmoid(prior_ref[:, 1, :])
    denominator = storage * (1.0 - weighting) + 0.5
    now = (0.5 - storage * weighting) / denominator
    back = (0.5 + storage * weighting) / denominator
    carry = (storage * (1.0 - weighting) - 0.5) / denominator
    echo = back + carry * now
    counts = jnp.broadcast_to(meta[2:3, :], (GROUP, LANES))
    stacked = [now, back, carry]
    stacked += [0.2 * prior_ref[:, 2 + order, :] for order in range(6)]
    stacked += [counts]
    stacked += [jnp.zeros((LANES - GROUP * len(stacked), LANES), jnp.float32)]
    columns = jnp.concatenate(stacked, axis=0).T
    lane_ids = lax.broadcasted_iota(jnp.int32, (LANES, LANES), 1).astype(jnp.float32)
    live = lane_ids < column(columns, 9 * GROUP)
    start_in = jnp.where(live, in_ref[...], 0.0)
    start_out = jnp.where(live, out_ref[...], 0.0)
    first_drain = drain_matrix(meta[0:1, :])
    second_drain = drain_matrix(meta[1:2, :])
    block_rows, lane_rows = gauge_places(meta)
    for member in range(GROUP):
        exponent = column(columns, 3 * GROUP + member) * modes_ref[0:1, :]
        for order in range(1, 6):
            exponent += column(columns, (3 + order) * GROUP + member) * modes_ref[order : order + 1, :]
        scaling = jnp.where(live, jnp.exp(exponent), 0.0)
        now_m = column(columns, member)
        back_m = column(columns, GROUP + member)
        carry_m = column(columns, 2 * GROUP + member)
        side0 = lateral_ref[member, pl.ds(0, LANES, stride=2), :] * scaling
        side1 = lateral_ref[member, pl.ds(1, LANES, stride=2), :] * scaling
        steady = back_m * start_in + carry_m * start_out
        passed = None
        flows = []
        for level, matrix in ((0, first_drain), (1, second_drain)):
            part = slice(level * BLK_LEV, (level + 1) * BLK_LEV)
            inflow0, inflow1 = side0[part], side1[part]
            if passed is not None:
                inflow0 += jnp.where(live[part], passed[:, :LANES], 0.0)
                inflow1 += jnp.where(live[part], passed[:, LANES:], 0.0)
            outflow0 = now_m[part] * inflow0 + steady[part]
            outflow1 = now_m[part] * inflow1 + back_m[part] * inflow0 + carry_m[part] * outflow0
            passed = drain(matrix, jnp.concatenate([outflow0, outflow1], axis=1))
            flows.append((outflow0, outflow1))
        for hour in range(2):
            first_row = ((member % 2) * 2 + hour) * BLK_LEV
            send_ref[member // 2, first_row : first_row + BLK_LEV, :] = passed[
                :, hour * LANES : (hour + 1) * LANES
            ]
            whole = jnp.concatenate([flows[0][hour], flows[1][hour]], axis=0)
            local_ref[member, hour * 4 : hour * 4 + 4, :] = read_gauges(whole, block_rows, lane_rows)
    for pair in range(GROUP // 2):
        send_ref[pair, FLOW_ROWS : FLOW_ROWS + 8, :] = jnp.concatenate(
            [
                now[2 * pair : 2 * pair + 2],
                echo[2 * pair : 2 * pair + 2],
                meta[2:3],
                jnp.zeros((3, LANES), jnp.float32),
            ],
            axis=0,
        )
        send_ref[pair, FLOW_ROWS + 8 : FLOW_ROWS + 16, :] = meta


def cascade_kernel(got_ref, out_ref):
    sources = got_ref.shape[0]
    coefs = [got_ref[source, FLOW_ROWS : FLOW_ROWS + 8, :] for source in range(sources)]
    columns = jnp.concatenate(coefs, axis=0).T
    lane_ids = lax.broadcasted_iota(jnp.int32, (LANES, LANES), 1).astype(jnp.float32)

    def flow(source):
        parts = [
            got_ref[source, (member * 2 + hour) * BLK_LEV : (member * 2 + hour + 1) * BLK_LEV, :]
            for hour in range(2)
            for member in range(2)
        ]
        return jnp.concatenate(parts, axis=1)

    out_ref[0] = jnp.zeros(out_ref.shape[1:], jnp.float32)
    upstream = flow(0)
    for source in range(1, sources):
        meta = got_ref[source, FLOW_ROWS + 8 : FLOW_ROWS + 16, :]
        live = lane_ids < column(columns, 8 * source + 4)
        now = [jnp.where(live, column(columns, 8 * source + member), 0.0) for member in range(2)]
        echo = [jnp.where(live, column(columns, 8 * source + 2 + member), 0.0) for member in range(2)]
        routed = []
        for level in range(2):
            part = slice(level * BLK_LEV, (level + 1) * BLK_LEV)
            first = [now[m][part] * upstream[:, m * LANES : (m + 1) * LANES] for m in range(2)]
            second = [
                now[m][part] * upstream[:, (2 + m) * LANES : (3 + m) * LANES]
                + echo[m][part] * upstream[:, m * LANES : (m + 1) * LANES]
                for m in range(2)
            ]
            routed.append(first + second)
            if level == 0 or source < sources - 1:
                upstream = drain(
                    drain_matrix(meta[level : level + 1, :]), jnp.concatenate(first + second, axis=1)
                )
        if source < sources - 1:
            upstream += flow(source)
        block_rows, lane_rows = gauge_places(meta)
        for member in range(2):
            for hour in range(2):
                whole = jnp.concatenate(
                    [routed[0][hour * 2 + member], routed[1][hour * 2 + member]], axis=0
                )
                first_row = (member * 2 + hour) * 4
                out_ref[source, first_row : first_row + 4, :] = read_gauges(
                    whole, block_rows, lane_rows
                )


def predicted_outflow(
    prior_params, lateral_flow, inflow_start, outflow_start, reach_count, downstream, gauge_reach
):
    members_dev, param_count, block_dev = prior_params.shape
    basins = lax.axis_size("basin")
    drains = downstream.reshape(2, BLK_LEV)
    meta = jnp.concatenate(
        [
            jnp.concatenate([drains, drains], axis=1),
            reach_count.reshape(1, block_dev),
            gauge_reach.reshape(4, LANES),
            jnp.zeros((1, LANES), jnp.int32),
        ],
        axis=0,
    ).astype(jnp.float32)
    orders = np.arange(8)[:, None]
    modes = np.cos(math.pi * orders * (np.arange(LANES)[None, :] + 0.5) / LANES).astype(np.float32)
    lateral_rows = (
        lateral_flow.reshape(members_dev, 2, block_dev, LANES)
        .transpose(0, 2, 1, 3)
        .reshape(members_dev, 2 * block_dev, LANES)
    )
    whole = lambda step: (0, 0)
    sent, local = pl.pallas_call(
        local_kernel,
        grid=(members_dev // GROUP,),
        in_specs=[
            pl.BlockSpec((GROUP, param_count, LANES), lambda step: (step, 0, 0)),
            pl.BlockSpec((GROUP, 2 * block_dev, LANES), lambda step: (step, 0, 0)),
            pl.BlockSpec((block_dev, LANES), whole),
            pl.BlockSpec((block_dev, LANES), whole),
            pl.BlockSpec((8, LANES), whole),
            pl.BlockSpec((8, LANES), whole),
        ],
        out_specs=[
            pl.BlockSpec((GROUP // 2, SEND_ROWS, LANES), lambda step: (step, 0, 0)),
            pl.BlockSpec((GROUP, 8, LANES), lambda step: (step, 0, 0)),
        ],
        out_shape=[
            jax.ShapeDtypeStruct((members_dev // 2, SEND_ROWS, LANES), jnp.float32),
            jax.ShapeDtypeStruct((members_dev, 8, LANES), jnp.float32),
        ],
        compiler_params=pltpu.CompilerParams(vmem_limit_bytes=40 * 2**20),
    )(
        prior_params,
        lateral_rows,
        inflow_start.reshape(block_dev, LANES),
        outflow_start.reshape(block_dev, LANES),
        meta,
        jnp.asarray(modes),
    )
    got = lax.all_to_all(sent, "basin", 0, 0, tiled=True)
    extra = pl.pallas_call(
        cascade_kernel,
        out_shape=jax.ShapeDtypeStruct((basins, 16, LANES), jnp.float32),
        compiler_params=pltpu.CompilerParams(vmem_limit_bytes=40 * 2**20),
    )(got)
    extra = lax.all_to_all(extra, "basin", 0, 0, tiled=True)
    return local + extra.reshape(members_dev, 8, LANES)


def solve_gram(gram_matrix, cross_matrix):
    factor = jnp.linalg.cholesky(gram_matrix)
    halfway = lax.linalg.triangular_solve(factor, cross_matrix, left_side=True, lower=True)
    return lax.linalg.triangular_solve(
        factor, halfway, left_side=True, lower=True, transpose_a=True
    )


def basin_sum(values):
    basins = lax.axis_size("basin")
    rows, width = values.shape
    pieces = values.reshape(basins, rows // basins, width)
    summed = jnp.sum(lax.all_to_all(pieces, "basin", 0, 0, tiled=True), axis=0)
    spread = jnp.broadcast_to(summed[None], (basins,) + summed.shape)
    return lax.all_to_all(spread, "basin", 0, 0, tiled=True).reshape(rows, width)


def shards(
    prior_params,
    lateral_flow,
    inflow_start,
    outflow_start,
    reach_count,
    downstream,
    gauge_reach,
    observed,
    obs_var,
    obs_noise,
):
    members_dev, param_count, block_dev = prior_params.shape
    members = members_dev * lax.axis_size("member")
    spread_root = math.sqrt(members - 1.0)
    prior_all = lax.all_gather(prior_params, "member", axis=0, tiled=True)
    outflow = predicted_outflow(
        prior_params, lateral_flow, inflow_start, outflow_start, reach_count, downstream, gauge_reach
    )
    predicted = inverse_sinh(outflow).reshape(members_dev, -1)
    spread = jnp.sqrt(obs_var).reshape(1, -1)
    innovation = (
        observed.reshape(1, -1) + 2.0 * spread * obs_noise.reshape(members_dev, -1) - predicted
    ) / (2.0 * spread)
    predicted_all = lax.all_gather(predicted, "member", axis=0, tiled=True)
    mean_pred = jnp.sum(predicted_all, 0) / members
    scaled_rows = (predicted_all - mean_pred) / (spread_root * (2.0 * spread))
    gram_part = jnp.dot(
        scaled_rows, scaled_rows.T, precision=exact_mode, preferred_element_type=jnp.float32
    )
    cross_part = jnp.dot(
        scaled_rows, innovation.T, precision=exact_mode, preferred_element_type=jnp.float32
    )
    cross_wide = jnp.concatenate([cross_part, jnp.zeros((members, LANES - members_dev), jnp.float32)], axis=1)
    both = basin_sum(jnp.concatenate([gram_part, cross_wide], axis=1))
    gram_matrix = both[:, :members] + jnp.eye(members, dtype=jnp.float32)
    solved = solve_gram(gram_matrix, both[:, members : members + members_dev])
    mean_prior = jnp.sum(prior_all, 0) / members
    anomaly = (prior_all - mean_prior) / spread_root
    posterior = prior_params + jnp.einsum("mn,mkb->nkb", solved, anomaly, precision=exact_mode)
    return (posterior, predicted.reshape(members_dev, 2, -1))


def solution(mesh):
    return jax.shard_map(
        shards,
        mesh=mesh,
        in_specs=(
            P("member", None, "basin"),
            P("member", None, "basin"),
            P("basin"),
            P("basin"),
            P("basin"),
            P("basin"),
            P("basin"),
            P(None, "basin"),
            P(None, "basin"),
            P("member", None, "basin"),
        ),
        out_specs=(P("member", None, "basin"), P("member", None, "basin")),
        check_vma=False,
    )
```

```python
import math

import jax
import jax.numpy as jnp
import numpy as np
from jax import lax
from jax.experimental import pallas as pl
from jax.experimental.pallas import tpu as pltpu
from jax.sharding import PartitionSpec as P

LANES = 128
BLK_LEV = 64
GROUP = 8
FLOW_ROWS = 256
SEND_ROWS = 272

exact_mode = lax.Precision.HIGHEST


def inverse_sinh(values):
    return jnp.log(values + jnp.sqrt(values * values + 1.0))


def two_terms(values):
    high = values.astype(jnp.bfloat16)
    low = (values - high.astype(jnp.float32)).astype(jnp.bfloat16)
    return jnp.concatenate([high, low], axis=0)


def drain_matrix(target_row):
    rows = lax.broadcasted_iota(jnp.int32, (BLK_LEV, LANES), 0).astype(jnp.float32)
    return jnp.where(rows == target_row, 1.0, 0.0).astype(jnp.bfloat16)


def drain(matrix, flows):
    return jnp.dot(matrix, two_terms(flows), preferred_element_type=jnp.float32)


def column(matrix, index):
    return jnp.broadcast_to(matrix[:, index : index + 1], (matrix.shape[0], LANES))


def wide(rows):
    return jnp.concatenate([rows[q : q + 1, :] for q in range(rows.shape[0])], axis=1)


def side_by_side(values):
    high = values.astype(jnp.bfloat16)
    return jnp.concatenate([high, (values - high.astype(jnp.float32)).astype(jnp.bfloat16)], axis=1)


def gauge_places(slot_rows):
    slots = wide(slot_rows).astype(jnp.int32)
    rows = lax.broadcasted_iota(jnp.int32, (LANES, slots.shape[1]), 0)
    picks = jnp.where(rows == (slots & 127), 1.0, 0.0).astype(jnp.bfloat16)
    return slots >> 7, jnp.concatenate([picks, picks], axis=0)


def read_gauges(flows, block_row, picks):
    picked = jnp.dot(side_by_side(flows), picks, preferred_element_type=jnp.float32)
    rows = lax.broadcasted_iota(jnp.int32, (LANES, picked.shape[1]), 0)
    mine = rows == block_row
    return [
        jnp.sum(jnp.where(mine, picked[first : first + LANES], 0.0), axis=0, keepdims=True)
        for first in range(0, flows.shape[0], LANES)
    ]


def gauge_rows(per_hour):
    return jnp.concatenate(
        [row[:, c * LANES : (c + 1) * LANES] for c in range(4) for row in per_hour], axis=0
    )


def local_kernel(
    prior_ref, lateral_ref, in_ref, out_ref, down_ref, count_ref, slot_ref, modes_ref, send_ref, local_ref
):
    down = jnp.broadcast_to(down_ref[...], (8, LANES)).astype(jnp.float32)
    turned = pltpu.roll(down, BLK_LEV, 1)
    left = lax.broadcasted_iota(jnp.int32, (8, LANES), 1) < BLK_LEV
    meta = jnp.concatenate(
        [
            jnp.where(left, down, turned)[:1],
            jnp.where(left, turned, down)[:1],
            count_ref[...].astype(jnp.float32),
            slot_ref[...].astype(jnp.float32),
            jnp.zeros((1, LANES), jnp.float32),
        ],
        axis=0,
    )
    storage = 0.02 + 0.1 * jax.nn.sigmoid(prior_ref[:, 0, :])
    weighting = 0.2 * jax.nn.sigmoid(prior_ref[:, 1, :])
    denominator = storage * (1.0 - weighting) + 0.5
    now = (0.5 - storage * weighting) / denominator
    back = (0.5 + storage * weighting) / denominator
    carry = (storage * (1.0 - weighting) - 0.5) / denominator
    echo = back + carry * now
    counts = jnp.broadcast_to(meta[2:3, :], (GROUP, LANES))
    stacked = [now, back, carry]
    stacked += [0.2 * prior_ref[:, 2 + order, :] for order in range(6)]
    stacked += [counts]
    stacked += [jnp.zeros((LANES - GROUP * len(stacked), LANES), jnp.float32)]
    columns = jnp.concatenate(stacked, axis=0).T
    lane_ids = lax.broadcasted_iota(jnp.int32, (LANES, LANES), 1).astype(jnp.float32)
    live = lane_ids < column(columns, 9 * GROUP)
    start_in = jnp.where(live, in_ref[...], 0.0)
    start_out = jnp.where(live, out_ref[...], 0.0)
    first_drain = drain_matrix(meta[0:1, :])
    second_drain = drain_matrix(meta[1:2, :])
    block_row, picks = gauge_places(meta[3:7])
    for member in range(GROUP):
        exponent = column(columns, 3 * GROUP + member) * modes_ref[0:1, :]
        for order in range(1, 6):
            exponent += column(columns, (3 + order) * GROUP + member) * modes_ref[order : order + 1, :]
        scaling = jnp.where(live, jnp.exp(exponent), 0.0)
        now_m = column(columns, member)
        back_m = column(columns, GROUP + member)
        carry_m = column(columns, 2 * GROUP + member)
        side0 = lateral_ref[member, pl.ds(0, LANES, stride=2), :] * scaling
        side1 = lateral_ref[member, pl.ds(1, LANES, stride=2), :] * scaling
        steady = back_m * start_in + carry_m * start_out
        passed = None
        flows = []
        for level, matrix in ((0, first_drain), (1, second_drain)):
            part = slice(level * BLK_LEV, (level + 1) * BLK_LEV)
            inflow0, inflow1 = side0[part], side1[part]
            if passed is not None:
                inflow0 += jnp.where(live[part], passed[:, :LANES], 0.0)
                inflow1 += jnp.where(live[part], passed[:, LANES:], 0.0)
            outflow0 = now_m[part] * inflow0 + steady[part]
            outflow1 = now_m[part] * inflow1 + back_m[part] * inflow0 + carry_m[part] * outflow0
            passed = drain(matrix, jnp.concatenate([outflow0, outflow1], axis=1))
            flows.append((outflow0, outflow1))
        for hour in range(2):
            first_row = ((member % 2) * 2 + hour) * BLK_LEV
            send_ref[member // 2, first_row : first_row + BLK_LEV, :] = passed[
                :, hour * LANES : (hour + 1) * LANES
            ]
        whole = jnp.concatenate([flows[level][hour] for hour in range(2) for level in range(2)], axis=0)
        local_ref[member] = gauge_rows(read_gauges(whole, block_row, picks))
    for pair in range(GROUP // 2):
        send_ref[pair, FLOW_ROWS : FLOW_ROWS + 8, :] = jnp.concatenate(
            [
                now[2 * pair : 2 * pair + 2],
                echo[2 * pair : 2 * pair + 2],
                meta[2:3],
                jnp.zeros((3, LANES), jnp.float32),
            ],
            axis=0,
        )
        send_ref[pair, FLOW_ROWS + 8 : FLOW_ROWS + 16, :] = meta


def cascade_kernel(got_ref, out_ref):
    sources = got_ref.shape[0]
    coefs = [got_ref[source, FLOW_ROWS : FLOW_ROWS + 8, :] for source in range(sources)]
    columns = jnp.concatenate(coefs, axis=0).T
    lane_ids = lax.broadcasted_iota(jnp.int32, (LANES, LANES), 1).astype(jnp.float32)

    def flow(source):
        parts = [
            got_ref[source, (member * 2 + hour) * BLK_LEV : (member * 2 + hour + 1) * BLK_LEV, :]
            for hour in range(2)
            for member in range(2)
        ]
        return jnp.concatenate(parts, axis=1)

    out_ref[0] = jnp.zeros(out_ref.shape[1:], jnp.float32)
    upstream = flow(0)
    for source in range(1, sources):
        meta = got_ref[source, FLOW_ROWS + 8 : FLOW_ROWS + 16, :]
        live = lane_ids < column(columns, 8 * source + 4)
        now = [jnp.where(live, column(columns, 8 * source + member), 0.0) for member in range(2)]
        echo = [jnp.where(live, column(columns, 8 * source + 2 + member), 0.0) for member in range(2)]
        routed = []
        for level in range(2):
            part = slice(level * BLK_LEV, (level + 1) * BLK_LEV)
            first = [now[m][part] * upstream[:, m * LANES : (m + 1) * LANES] for m in range(2)]
            second = [
                now[m][part] * upstream[:, (2 + m) * LANES : (3 + m) * LANES]
                + echo[m][part] * upstream[:, m * LANES : (m + 1) * LANES]
                for m in range(2)
            ]
            routed.append(first + second)
            if level == 0 or source < sources - 1:
                upstream = drain(
                    drain_matrix(meta[level : level + 1, :]), jnp.concatenate(first + second, axis=1)
                )
        if source < sources - 1:
            upstream += flow(source)
        block_row, picks = gauge_places(meta[3:7])
        whole = jnp.concatenate(
            [
                routed[level][hour * 2 + member]
                for member in range(2)
                for hour in range(2)
                for level in range(2)
            ],
            axis=0,
        )
        read = read_gauges(whole, block_row, picks)
        out_ref[source] = jnp.concatenate([gauge_rows(read[:2]), gauge_rows(read[2:])], axis=0)


def predicted_outflow(
    prior_params, lateral_flow, inflow_start, outflow_start, reach_count, downstream, gauge_reach
):
    members_dev, param_count, block_dev = prior_params.shape
    basins = lax.axis_size("basin")
    orders = np.arange(8)[:, None]
    modes = np.cos(math.pi * orders * (np.arange(LANES)[None, :] + 0.5) / LANES).astype(np.float32)
    lateral_rows = (
        lateral_flow.reshape(members_dev, 2, block_dev, LANES)
        .transpose(0, 2, 1, 3)
        .reshape(members_dev, 2 * block_dev, LANES)
    )
    whole = lambda step: (0, 0)
    sent, local = pl.pallas_call(
        local_kernel,
        grid=(members_dev // GROUP,),
        in_specs=[
            pl.BlockSpec((GROUP, param_count, LANES), lambda step: (step, 0, 0)),
            pl.BlockSpec((GROUP, 2 * block_dev, LANES), lambda step: (step, 0, 0)),
            pl.BlockSpec((block_dev, LANES), whole),
            pl.BlockSpec((block_dev, LANES), whole),
            pl.BlockSpec((1, LANES), whole),
            pl.BlockSpec((1, LANES), whole),
            pl.BlockSpec((4, LANES), whole),
            pl.BlockSpec((8, LANES), whole),
        ],
        out_specs=[
            pl.BlockSpec((GROUP // 2, SEND_ROWS, LANES), lambda step: (step, 0, 0)),
            pl.BlockSpec((GROUP, 8, LANES), lambda step: (step, 0, 0)),
        ],
        out_shape=[
            jax.ShapeDtypeStruct((members_dev // 2, SEND_ROWS, LANES), jnp.float32),
            jax.ShapeDtypeStruct((members_dev, 8, LANES), jnp.float32),
        ],
        compiler_params=pltpu.CompilerParams(vmem_limit_bytes=60 * 2**20),
    )(
        prior_params,
        lateral_rows,
        inflow_start.reshape(block_dev, LANES),
        outflow_start.reshape(block_dev, LANES),
        downstream.reshape(1, block_dev),
        reach_count.reshape(1, block_dev),
        gauge_reach.reshape(4, LANES),
        jnp.asarray(modes),
    )
    got = lax.all_to_all(sent, "basin", 0, 0, tiled=True)
    extra = pl.pallas_call(
        cascade_kernel,
        out_shape=jax.ShapeDtypeStruct((basins, 16, LANES), jnp.float32),
        compiler_params=pltpu.CompilerParams(vmem_limit_bytes=40 * 2**20),
    )(got)
    extra = lax.all_to_all(extra, "basin", 0, 0, tiled=True)
    return local + extra.reshape(members_dev, 8, LANES)


def full(row, lane):
    return jnp.broadcast_to(row[:, lane : lane + 1], (8, LANES))

def product(a, b):
    return [
        [sum_terms([a[i][k] * b[k][j] for k in range(len(b))]) for j in range(len(b[0]))]
        for i in range(len(a))
    ]


def sum_terms(terms):
    while len(terms) > 1:
        terms = [terms[i] + terms[i + 1] for i in range(0, len(terms), 2)]
    return terms[0]


def flipped(a):
    return [list(row) for row in zip(*a)]


def symmetric_inverse(p):
    half = len(p) // 2
    if len(p) == 2:
        scale = 1.0 / (p[0][0] * p[1][1] - p[0][1] * p[0][1])
        cross = -p[0][1] * scale
        return [[p[1][1] * scale, cross], [cross, p[0][0] * scale]]
    corner = [row[half:] for row in p[:half]]
    first = symmetric_inverse([row[:half] for row in p[:half]])
    lifted = product(first, corner)
    shift = product(flipped(corner), lifted)
    second = symmetric_inverse(
        [[p[half + i][half + j] - shift[i][j] for j in range(half)] for i in range(half)]
    )
    moved = product(lifted, second)
    back = product(moved, flipped(lifted))
    top = [
        [first[i][j] + back[i][j] for j in range(half)] + [-moved[i][j] for j in range(half)]
        for i in range(half)
    ]
    low = [[-moved[j][i] for j in range(half)] + second[i] for i in range(half)]
    return top + low


PIVOT = 8


def invert_block(block):
    tiles = [block[8 * t : 8 * t + 8, :] for t in range(16)]
    lanes = lax.broadcasted_iota(jnp.int32, (8, LANES), 1)
    subs = lax.broadcasted_iota(jnp.int32, (8, LANES), 0)
    for first in range(0, LANES, PIVOT):
        home, offset = first // 8, first % 8
        rows = [
            jnp.broadcast_to(tiles[home][offset + i : offset + i + 1, :], (8, LANES))
            for i in range(PIVOT)
        ]
        pivots = [
            [full(rows[min(i, j)], first + max(i, j)) if i <= j else None for j in range(PIVOT)]
            for i in range(PIVOT)
        ]
        pivots = [[pivots[min(i, j)][max(i, j)] for j in range(PIVOT)] for i in range(PIVOT)]
        inverse = symmetric_inverse(pivots)
        group = (lanes >= first) & (lanes < first + PIVOT)
        units = [
            jnp.where(group, jnp.where(lanes == first + i, 1.0, 0.0), rows[i]) for i in range(PIVOT)
        ]
        fresh = [sum_terms([inverse[i][j] * units[j] for j in range(PIVOT)]) for i in range(PIVOT)]
        for t in range(16):
            cols = [full(tiles[t], first + i) for i in range(PIVOT)]
            updated = jnp.where(group, 0.0, tiles[t]) - sum_terms(
                [cols[i] * fresh[i] for i in range(PIVOT)]
            )
            if t == home:
                for i in range(PIVOT):
                    updated = jnp.where(subs == offset + i, fresh[i], updated)
            tiles[t] = updated
    return jnp.concatenate(tiles, axis=0)


def exact_dot(a, b):
    return jnp.dot(a, b, precision=exact_mode, preferred_element_type=jnp.float32)


UPPER = (((0, 0), (0, 1), (0, 2), (0, 3), (1, 1)), ((1, 2), (1, 3), (2, 2), (2, 3), (3, 3)))


def rows_of(index):
    return slice(index * LANES, (index + 1) * LANES)


def split(values):
    high = values.astype(jnp.bfloat16)
    return high, (values - high.astype(jnp.float32)).astype(jnp.bfloat16)


def pair_dot(left, right):
    rows = left[0].shape[0]
    stacked = jnp.concatenate(left, axis=0)
    high, low = [
        lax.dot_general(
            stacked, part, (((1,), (1,)), ((), ())), preferred_element_type=jnp.float32
        )
        for part in right
    ]
    return high[:rows] + (high[rows:] + low[:rows]) + low[rows:]


def gram_kernel(place_ref, *refs):
    pieces, (noise_ref, observed_ref, var_ref, out_ref, rows_ref, high_ref, low_ref) = (
        refs[:16],
        refs[16:],
    )
    zone, core = place_ref[0], place_ref[1]
    members_dev = noise_ref.shape[0]
    members, width = rows_ref.shape
    for piece, ref in enumerate(pieces):
        ring = piece % 8
        owner = lax.rem(zone + ring + 4, 8) * 2 + (core if piece < 8 else 1 - core)
        first = pl.multiple_of(owner * members_dev, members_dev)
        for q in range(8):
            rows_ref[pl.ds(first, members_dev), q * LANES : (q + 1) * LANES] = ref[:, q, :]
    spread = 2.0 * jnp.sqrt(wide(var_ref[...]))
    mean = jnp.sum(rows_ref[...], axis=0, keepdims=True) / members
    own = jnp.concatenate([pieces[4][:, q, :] for q in range(8)], axis=1)
    noise = jnp.concatenate([noise_ref[:, q, :] for q in range(8)], axis=1)
    innovation = (wide(observed_ref[...]) + spread * noise - own) / spread
    scale = 1.0 / (math.sqrt(members - 1.0) * spread)
    high_ref[...], low_ref[...] = split((rows_ref[...] - mean) * scale)
    crossed = pair_dot(split(innovation), (high_ref[...], low_ref[...]))
    for c in range(4):
        first = 5 * LANES + c * members_dev
        out_ref[first : first + members_dev, :] = crossed[:, rows_of(c)]

    def fill(position, row, first_col, last_col):
        columns = slice(first_col * LANES, (last_col + 1) * LANES)
        product = pair_dot(
            (high_ref[rows_of(row), :], low_ref[rows_of(row), :]),
            (high_ref[columns, :], low_ref[columns, :]),
        )
        for c in range(last_col - first_col + 1):
            out_ref[rows_of(position + c), :] = product[:, rows_of(c)]

    @pl.when(core == 0)
    def _():
        fill(0, 0, 0, 3)
        fill(4, 1, 1, 1)

    @pl.when(core == 1)
    def _():
        fill(0, 1, 2, 3)
        fill(2, 2, 2, 3)
        fill(4, 3, 3, 3)


def sum_kernel(parts_ref, out_ref):
    total = parts_ref[0]
    for source in range(1, parts_ref.shape[0]):
        total += parts_ref[source]
    for target in range(out_ref.shape[0]):
        out_ref[target] = total


def solve_kernel(place_ref, own_ref, other_ref, prior_ref, all_ref, out_ref, work_ref):
    core = place_ref[1]
    size = work_ref.shape[0]
    count = size // LANES
    members_dev = LANES // 4

    def fill(pairs, ref):
        for position, (r, c) in enumerate(pairs):
            block = ref[rows_of(position), :]
            work_ref[rows_of(r), rows_of(c)] = block
            if r != c:
                work_ref[rows_of(c), rows_of(r)] = block.T

    @pl.when(core == 0)
    def _():
        fill(UPPER[0], own_ref)
        fill(UPPER[1], other_ref)

    @pl.when(core == 1)
    def _():
        fill(UPPER[0], other_ref)
        fill(UPPER[1], own_ref)

    crossed = own_ref[5 * LANES : 6 * LANES, :].T
    for r in range(count):
        work_ref[rows_of(r), size : size + members_dev] = crossed[
            :, r * members_dev : (r + 1) * members_dev
        ]
        work_ref[rows_of(r), size + members_dev :] = jnp.zeros(
            (LANES, LANES - members_dev), jnp.float32
        )
    diagonal = lax.broadcasted_iota(jnp.int32, (LANES, LANES), 0) == lax.broadcasted_iota(
        jnp.int32, (LANES, LANES), 1
    )
    unit = jnp.where(diagonal, 1.0, 0.0)
    for k in range(count):
        inverse = invert_block(work_ref[rows_of(k), rows_of(k)] + unit)
        rest = slice((k + 1) * LANES, size + LANES)
        scaled = exact_dot(inverse, work_ref[rows_of(k), rest])
        for r in range(count):
            if r != k:
                work_ref[rows_of(r), rest] -= exact_dot(work_ref[rows_of(r), rows_of(k)], scaled)
        work_ref[rows_of(k), rest] = scaled
    gain = work_ref[:, size:]
    gain = (gain - jnp.sum(gain, axis=0, keepdims=True) / size) / math.sqrt(size - 1.0)
    turned = jnp.concatenate([gain[rows_of(r)].T for r in range(count)], axis=1)[:members_dev]
    high, low = split(turned)
    both = jnp.concatenate([high, low], axis=0)
    for order in range(prior_ref.shape[1]):
        all_high, all_low = split(all_ref[:, order, :])
        first = jnp.dot(both, all_high, preferred_element_type=jnp.float32)
        second = jnp.dot(high, all_low, preferred_element_type=jnp.float32)
        out_ref[:, order, :] = prior_ref[:, order, :] + (
            first[:members_dev] + (first[members_dev:] + second)
        )


def ring_pieces(values):
    count = lax.axis_size("member")
    turn = lambda x, step: lax.ppermute(
        x, "member", [(i, (i + 2 * step) % count) for i in range(count)]
    )
    swap = lambda x: lax.ppermute(x, "member", [(i, i ^ 1) for i in range(count)])
    below, above = [values], [values]
    for step in range(1, 5):
        below.append(turn(below[-1], 1))
        if step < 4:
            above.append(turn(above[-1], -1))
    pieces = below[:0:-1] + above
    return pieces + [swap(piece) for piece in pieces], swap


def by_chunk(values):
    return values.reshape(-1, 2, 4, LANES).transpose(0, 2, 1, 3).reshape(-1, 8, LANES)


def by_hour(values):
    return values.reshape(-1, 4, 2, LANES).transpose(0, 2, 1, 3).reshape(-1, 2, 4 * LANES)


def shards(
    prior_params,
    lateral_flow,
    inflow_start,
    outflow_start,
    reach_count,
    downstream,
    gauge_reach,
    observed,
    obs_var,
    obs_noise,
):
    members_dev, param_count, block_dev = prior_params.shape
    members = members_dev * lax.axis_size("member")
    basins = lax.axis_size("basin")
    member_idx = lax.axis_index("member")
    place = jnp.stack([member_idx // 2, member_idx % 2]).astype(jnp.int32)
    scalars = pl.BlockSpec(memory_space=pltpu.SMEM)
    dense = pl.BlockSpec(memory_space=pltpu.VMEM)
    big = pltpu.CompilerParams(vmem_limit_bytes=40 * 2**20)
    prior_all = lax.all_gather(prior_params, "member", axis=0, tiled=True)
    outflow = predicted_outflow(
        prior_params, lateral_flow, inflow_start, outflow_start, reach_count, downstream, gauge_reach
    )
    predicted = inverse_sinh(outflow)
    pieces, swap = ring_pieces(predicted)
    part = pl.pallas_call(
        gram_kernel,
        in_specs=[scalars] + [dense] * 19,
        out_specs=dense,
        out_shape=jax.ShapeDtypeStruct((6 * LANES, LANES), jnp.float32),
        scratch_shapes=[
            pltpu.VMEM((members, 8 * LANES), jnp.float32),
            pltpu.VMEM((members, 8 * LANES), jnp.bfloat16),
            pltpu.VMEM((members, 8 * LANES), jnp.bfloat16),
        ],
        compiler_params=big,
    )(
        place,
        *pieces,
        by_chunk(obs_noise),
        by_chunk(observed[None])[0],
        by_chunk(obs_var[None])[0],
    )
    part = lax.all_to_all(part.reshape(basins, -1, LANES), "basin", 0, 0, tiled=True)
    summed = pl.pallas_call(
        sum_kernel, out_shape=jax.ShapeDtypeStruct(part.shape, jnp.float32), compiler_params=big
    )(part)
    own = lax.all_to_all(summed, "basin", 0, 0, tiled=True).reshape(6 * LANES, LANES)
    other = swap(own[: 5 * LANES])
    posterior = pl.pallas_call(
        solve_kernel,
        in_specs=[scalars] + [dense] * 4,
        out_specs=dense,
        out_shape=jax.ShapeDtypeStruct(prior_params.shape, jnp.float32),
        scratch_shapes=[pltpu.VMEM((members, members + LANES), jnp.float32)],
        compiler_params=big,
    )(place, own, other, prior_params, prior_all)
    return (posterior, by_hour(predicted))


def solution(mesh):
    return jax.shard_map(
        shards,
        mesh=mesh,
        in_specs=(
            P("member", None, "basin"),
            P("member", None, "basin"),
            P("basin"),
            P("basin"),
            P("basin"),
            P("basin"),
            P("basin"),
            P(None, "basin"),
            P(None, "basin"),
            P("member", None, "basin"),
        ),
        out_specs=(P("member", None, "basin"), P("member", None, "basin")),
        check_vma=False,
    )
```

```python
import functools
import math

import jax
import jax.numpy as jnp
import numpy as np
from jax import lax
from jax.experimental import pallas as pl
from jax.experimental.pallas import tpu as pltpu
from jax.sharding import PartitionSpec as P

LANES = 128
BLK_LEV = 64
GROUP = 8
FLOW_ROWS = 256
SEND_ROWS = 272

exact_mode = lax.Precision.HIGHEST


def inverse_sinh(values):
    return jnp.log(values + jnp.sqrt(values * values + 1.0))


def two_terms(values):
    high = values.astype(jnp.bfloat16)
    low = (values - high.astype(jnp.float32)).astype(jnp.bfloat16)
    return jnp.concatenate([high, low], axis=0)


def drain_matrix(target_row):
    rows = lax.broadcasted_iota(jnp.int32, (BLK_LEV, LANES), 0).astype(jnp.float32)
    return jnp.where(rows == target_row, 1.0, 0.0).astype(jnp.bfloat16)


def drain(matrix, flows):
    return jnp.dot(matrix, two_terms(flows), preferred_element_type=jnp.float32)


def column(matrix, index):
    return jnp.broadcast_to(matrix[:, index : index + 1], (matrix.shape[0], LANES))


def wide(rows):
    return jnp.concatenate([rows[q : q + 1, :] for q in range(rows.shape[0])], axis=1)


def side_by_side(values):
    high = values.astype(jnp.bfloat16)
    return jnp.concatenate([high, (values - high.astype(jnp.float32)).astype(jnp.bfloat16)], axis=1)


def gauge_places(slot_rows):
    slots = wide(slot_rows).astype(jnp.int32)
    rows = lax.broadcasted_iota(jnp.int32, (LANES, slots.shape[1]), 0)
    picks = jnp.where(rows == (slots & 127), 1.0, 0.0).astype(jnp.bfloat16)
    return slots >> 7, jnp.concatenate([picks, picks], axis=0)


def read_gauges(flows, block_row, picks):
    picked = jnp.dot(side_by_side(flows), picks, preferred_element_type=jnp.float32)
    rows = lax.broadcasted_iota(jnp.int32, (LANES, picked.shape[1]), 0)
    mine = rows == block_row
    return [
        jnp.sum(jnp.where(mine, picked[first : first + LANES], 0.0), axis=0, keepdims=True)
        for first in range(0, flows.shape[0], LANES)
    ]


def gauge_rows(per_hour):
    return jnp.concatenate(
        [row[:, c * LANES : (c + 1) * LANES] for c in range(4) for row in per_hour], axis=0
    )


def local_kernel(
    reads, prior_ref, lateral_ref, in_ref, out_ref, down_ref, count_ref, slot_ref, modes_ref, *rest
):
    result_ref = rest[-1]
    down = jnp.broadcast_to(down_ref[...], (8, LANES)).astype(jnp.float32)
    turned = pltpu.roll(down, BLK_LEV, 1)
    left = lax.broadcasted_iota(jnp.int32, (8, LANES), 1) < BLK_LEV
    meta = jnp.concatenate(
        [
            jnp.where(left, down, turned)[:1],
            jnp.where(left, turned, down)[:1],
            count_ref[...].astype(jnp.float32),
            slot_ref[...].astype(jnp.float32),
            jnp.zeros((1, LANES), jnp.float32),
        ],
        axis=0,
    )
    storage = 0.02 + 0.1 * jax.nn.sigmoid(prior_ref[:, 0, :])
    weighting = 0.2 * jax.nn.sigmoid(prior_ref[:, 1, :])
    denominator = storage * (1.0 - weighting) + 0.5
    now = (0.5 - storage * weighting) / denominator
    back = (0.5 + storage * weighting) / denominator
    carry = (storage * (1.0 - weighting) - 0.5) / denominator
    echo = back + carry * now
    counts = jnp.broadcast_to(meta[2:3, :], (GROUP, LANES))
    stacked = [now, back, carry]
    stacked += [0.2 * prior_ref[:, 2 + order, :] for order in range(6)]
    stacked += [counts]
    stacked += [jnp.zeros((LANES - GROUP * len(stacked), LANES), jnp.float32)]
    columns = jnp.concatenate(stacked, axis=0).T
    lane_ids = lax.broadcasted_iota(jnp.int32, (LANES, LANES), 1).astype(jnp.float32)
    live = lane_ids < column(columns, 9 * GROUP)
    start_in = jnp.where(live, in_ref[...], 0.0)
    start_out = jnp.where(live, out_ref[...], 0.0)
    first_drain = drain_matrix(meta[0:1, :])
    second_drain = drain_matrix(meta[1:2, :])
    if reads:
        block_row, picks = gauge_places(meta[3:7])
    for member in range(GROUP):
        exponent = column(columns, 3 * GROUP + member) * modes_ref[0:1, :]
        for order in range(1, 6):
            exponent += column(columns, (3 + order) * GROUP + member) * modes_ref[order : order + 1, :]
        scaling = jnp.where(live, jnp.exp(exponent), 0.0)
        now_m = column(columns, member)
        back_m = column(columns, GROUP + member)
        carry_m = column(columns, 2 * GROUP + member)
        side0 = lateral_ref[member, pl.ds(0, LANES, stride=2), :] * scaling
        side1 = lateral_ref[member, pl.ds(1, LANES, stride=2), :] * scaling
        steady = back_m * start_in + carry_m * start_out
        passed = None
        flows = []
        for level, matrix in ((0, first_drain), (1, second_drain)):
            part = slice(level * BLK_LEV, (level + 1) * BLK_LEV)
            inflow0, inflow1 = side0[part], side1[part]
            if passed is not None:
                inflow0 += jnp.where(live[part], passed[:, :LANES], 0.0)
                inflow1 += jnp.where(live[part], passed[:, LANES:], 0.0)
            outflow0 = now_m[part] * inflow0 + steady[part]
            outflow1 = now_m[part] * inflow1 + back_m[part] * inflow0 + carry_m[part] * outflow0
            if level == 0 or not reads:
                passed = drain(matrix, jnp.concatenate([outflow0, outflow1], axis=1))
            flows.append((outflow0, outflow1))
        if reads:
            whole = jnp.concatenate([flows[level][hour] for hour in range(2) for level in range(2)], axis=0)
            result_ref[member] = gauge_rows(read_gauges(whole, block_row, picks))
            continue
        for hour in range(2):
            first_row = ((member % 2) * 2 + hour) * BLK_LEV
            result_ref[member // 2, first_row : first_row + BLK_LEV, :] = passed[
                :, hour * LANES : (hour + 1) * LANES
            ]
    if reads:
        return
    for pair in range(GROUP // 2):
        result_ref[pair, FLOW_ROWS : FLOW_ROWS + 8, :] = jnp.concatenate(
            [
                now[2 * pair : 2 * pair + 2],
                echo[2 * pair : 2 * pair + 2],
                meta[2:3],
                jnp.zeros((3, LANES), jnp.float32),
            ],
            axis=0,
        )
        result_ref[pair, FLOW_ROWS + 8 : FLOW_ROWS + 16, :] = meta


def cascade_kernel(got_ref, _, out_ref):
    sources = got_ref.shape[0]
    coefs = [got_ref[source, FLOW_ROWS : FLOW_ROWS + 8, :] for source in range(sources)]
    columns = jnp.concatenate(coefs, axis=0).T
    lane_ids = lax.broadcasted_iota(jnp.int32, (LANES, LANES), 1).astype(jnp.float32)

    def flow(source):
        parts = [
            got_ref[source, (member * 2 + hour) * BLK_LEV : (member * 2 + hour + 1) * BLK_LEV, :]
            for hour in range(2)
            for member in range(2)
        ]
        return jnp.concatenate(parts, axis=1)

    out_ref[0] = jnp.zeros(out_ref.shape[1:], jnp.float32)
    upstream = flow(0)
    for source in range(1, sources):
        meta = got_ref[source, FLOW_ROWS + 8 : FLOW_ROWS + 16, :]
        live = lane_ids < column(columns, 8 * source + 4)
        now = [jnp.where(live, column(columns, 8 * source + member), 0.0) for member in range(2)]
        echo = [jnp.where(live, column(columns, 8 * source + 2 + member), 0.0) for member in range(2)]
        routed = []
        for level in range(2):
            part = slice(level * BLK_LEV, (level + 1) * BLK_LEV)
            first = [now[m][part] * upstream[:, m * LANES : (m + 1) * LANES] for m in range(2)]
            second = [
                now[m][part] * upstream[:, (2 + m) * LANES : (3 + m) * LANES]
                + echo[m][part] * upstream[:, m * LANES : (m + 1) * LANES]
                for m in range(2)
            ]
            routed.append(first + second)
            if level == 0 or source < sources - 1:
                upstream = drain(
                    drain_matrix(meta[level : level + 1, :]), jnp.concatenate(first + second, axis=1)
                )
        if source < sources - 1:
            upstream += flow(source)
        block_row, picks = gauge_places(meta[3:7])
        whole = jnp.concatenate(
            [
                routed[level][hour * 2 + member]
                for member in range(2)
                for hour in range(2)
                for level in range(2)
            ],
            axis=0,
        )
        read = read_gauges(whole, block_row, picks)
        out_ref[source] = jnp.concatenate([gauge_rows(read[:2]), gauge_rows(read[2:])], axis=0)


def predicted_outflow(
    prior_params, lateral_flow, inflow_start, outflow_start, reach_count, downstream, gauge_reach
):
    members_dev, param_count, block_dev = prior_params.shape
    basins = lax.axis_size("basin")
    orders = np.arange(8)[:, None]
    modes = np.cos(math.pi * orders * (np.arange(LANES)[None, :] + 0.5) / LANES).astype(np.float32)
    lateral_rows = (
        lateral_flow.reshape(members_dev, 2, block_dev, LANES)
        .transpose(0, 2, 1, 3)
        .reshape(members_dev, 2 * block_dev, LANES)
    )
    whole = lambda step: (0, 0)
    operands = (
        prior_params,
        lateral_rows,
        inflow_start.reshape(block_dev, LANES),
        outflow_start.reshape(block_dev, LANES),
        downstream.reshape(1, block_dev),
        reach_count.reshape(1, block_dev),
        gauge_reach.reshape(4, LANES),
        jnp.asarray(modes),
    )
    blocks = [
        pl.BlockSpec((GROUP, param_count, LANES), lambda step: (step, 0, 0)),
        pl.BlockSpec((GROUP, 2 * block_dev, LANES), lambda step: (step, 0, 0)),
        pl.BlockSpec((block_dev, LANES), whole),
        pl.BlockSpec((block_dev, LANES), whole),
        pl.BlockSpec((1, LANES), whole),
        pl.BlockSpec((1, LANES), whole),
        pl.BlockSpec((4, LANES), whole),
        pl.BlockSpec((8, LANES), whole),
    ]
    roomy = pltpu.CompilerParams(vmem_limit_bytes=60 * 2**20)
    sent = pl.pallas_call(
        functools.partial(local_kernel, False),
        grid=(members_dev // GROUP,),
        in_specs=blocks,
        out_specs=pl.BlockSpec((GROUP // 2, SEND_ROWS, LANES), lambda step: (step, 0, 0)),
        out_shape=jax.ShapeDtypeStruct((members_dev // 2, SEND_ROWS, LANES), jnp.float32),
        compiler_params=roomy,
    )(*operands)
    local = pl.pallas_call(
        functools.partial(local_kernel, True),
        grid=(members_dev // GROUP,),
        in_specs=blocks + [pl.BlockSpec((1, 8, LANES), lambda step: (0, 0, 0))],
        out_specs=pl.BlockSpec((GROUP, 8, LANES), lambda step: (step, 0, 0)),
        out_shape=jax.ShapeDtypeStruct((members_dev, 8, LANES), jnp.float32),
        compiler_params=roomy,
    )(*operands, sent)
    got = lax.all_to_all(sent, "basin", 0, 0, tiled=True)
    extra = pl.pallas_call(
        cascade_kernel,
        in_specs=[pl.BlockSpec(memory_space=pltpu.VMEM), pl.BlockSpec(memory_space=pltpu.HBM)],
        out_shape=jax.ShapeDtypeStruct((basins, 16, LANES), jnp.float32),
        compiler_params=pltpu.CompilerParams(vmem_limit_bytes=40 * 2**20),
    )(got, local)
    extra = lax.all_to_all(extra, "basin", 0, 0, tiled=True)
    return local + extra.reshape(members_dev, 8, LANES)


def full(row, lane):
    return jnp.broadcast_to(row[:, lane : lane + 1], (8, LANES))

def product(a, b):
    return [
        [sum_terms([a[i][k] * b[k][j] for k in range(len(b))]) for j in range(len(b[0]))]
        for i in range(len(a))
    ]


def sum_terms(terms):
    while len(terms) > 1:
        terms = [terms[i] + terms[i + 1] for i in range(0, len(terms), 2)]
    return terms[0]


def flipped(a):
    return [list(row) for row in zip(*a)]


def symmetric_inverse(p):
    half = len(p) // 2
    if len(p) == 2:
        scale = 1.0 / (p[0][0] * p[1][1] - p[0][1] * p[0][1])
        cross = -p[0][1] * scale
        return [[p[1][1] * scale, cross], [cross, p[0][0] * scale]]
    corner = [row[half:] for row in p[:half]]
    first = symmetric_inverse([row[:half] for row in p[:half]])
    lifted = product(first, corner)
    shift = product(flipped(corner), lifted)
    second = symmetric_inverse(
        [[p[half + i][half + j] - shift[i][j] for j in range(half)] for i in range(half)]
    )
    moved = product(lifted, second)
    back = product(moved, flipped(lifted))
    top = [
        [first[i][j] + back[i][j] for j in range(half)] + [-moved[i][j] for j in range(half)]
        for i in range(half)
    ]
    low = [[-moved[j][i] for j in range(half)] + second[i] for i in range(half)]
    return top + low


PIVOT = 8


def invert_block(block):
    tiles = [block[8 * t : 8 * t + 8, :] for t in range(16)]
    lanes = lax.broadcasted_iota(jnp.int32, (8, LANES), 1)
    subs = lax.broadcasted_iota(jnp.int32, (8, LANES), 0)
    for first in range(0, LANES, PIVOT):
        home, offset = first // 8, first % 8
        rows = [
            jnp.broadcast_to(tiles[home][offset + i : offset + i + 1, :], (8, LANES))
            for i in range(PIVOT)
        ]
        pivots = [
            [full(rows[min(i, j)], first + max(i, j)) if i <= j else None for j in range(PIVOT)]
            for i in range(PIVOT)
        ]
        pivots = [[pivots[min(i, j)][max(i, j)] for j in range(PIVOT)] for i in range(PIVOT)]
        inverse = symmetric_inverse(pivots)
        group = (lanes >= first) & (lanes < first + PIVOT)
        units = [
            jnp.where(group, jnp.where(lanes == first + i, 1.0, 0.0), rows[i]) for i in range(PIVOT)
        ]
        fresh = [sum_terms([inverse[i][j] * units[j] for j in range(PIVOT)]) for i in range(PIVOT)]
        for t in range(16):
            cols = [full(tiles[t], first + i) for i in range(PIVOT)]
            updated = jnp.where(group, 0.0, tiles[t]) - sum_terms(
                [cols[i] * fresh[i] for i in range(PIVOT)]
            )
            if t == home:
                for i in range(PIVOT):
                    updated = jnp.where(subs == offset + i, fresh[i], updated)
            tiles[t] = updated
    return jnp.concatenate(tiles, axis=0)


def exact_dot(a, b):
    return jnp.dot(a, b, precision=exact_mode, preferred_element_type=jnp.float32)


UPPER = (((0, 0), (0, 1), (0, 2), (0, 3), (1, 1)), ((1, 2), (1, 3), (2, 2), (2, 3), (3, 3)))


def rows_of(index):
    return slice(index * LANES, (index + 1) * LANES)


def split(values):
    high = values.astype(jnp.bfloat16)
    return high, (values - high.astype(jnp.float32)).astype(jnp.bfloat16)


def pair_dot(left, right):
    rows = left[0].shape[0]
    stacked = jnp.concatenate(left, axis=0)
    high, low = [
        lax.dot_general(
            stacked, part, (((1,), (1,)), ((), ())), preferred_element_type=jnp.float32
        )
        for part in right
    ]
    return high[:rows] + (high[rows:] + low[:rows]) + low[rows:]


def gram_kernel(place_ref, *refs):
    pieces, (noise_ref, observed_ref, var_ref, out_ref, rows_ref, high_ref, low_ref) = (
        refs[:16],
        refs[16:],
    )
    zone, core = place_ref[0], place_ref[1]
    members_dev = noise_ref.shape[0]
    members, width = rows_ref.shape
    for piece, ref in enumerate(pieces):
        ring = piece % 8
        owner = lax.rem(zone + ring + 4, 8) * 2 + (core if piece < 8 else 1 - core)
        first = pl.multiple_of(owner * members_dev, members_dev)
        for q in range(8):
            rows_ref[pl.ds(first, members_dev), q * LANES : (q + 1) * LANES] = ref[:, q, :]
    spread = 2.0 * jnp.sqrt(wide(var_ref[...]))
    mean = jnp.sum(rows_ref[...], axis=0, keepdims=True) / members
    own = jnp.concatenate([pieces[4][:, q, :] for q in range(8)], axis=1)
    noise = jnp.concatenate([noise_ref[:, q, :] for q in range(8)], axis=1)
    innovation = (wide(observed_ref[...]) + spread * noise - own) / spread
    scale = 1.0 / (math.sqrt(members - 1.0) * spread)
    high_ref[...], low_ref[...] = split((rows_ref[...] - mean) * scale)
    crossed = pair_dot(split(innovation), (high_ref[...], low_ref[...]))
    for c in range(4):
        first = 5 * LANES + c * members_dev
        out_ref[first : first + members_dev, :] = crossed[:, rows_of(c)]

    def fill(position, row, first_col, last_col):
        columns = slice(first_col * LANES, (last_col + 1) * LANES)
        product = pair_dot(
            (high_ref[rows_of(row), :], low_ref[rows_of(row), :]),
            (high_ref[columns, :], low_ref[columns, :]),
        )
        for c in range(last_col - first_col + 1):
            out_ref[rows_of(position + c), :] = product[:, rows_of(c)]

    @pl.when(core == 0)
    def _():
        fill(0, 0, 0, 3)
        fill(4, 1, 1, 1)

    @pl.when(core == 1)
    def _():
        fill(0, 1, 2, 3)
        fill(2, 2, 2, 3)
        fill(4, 3, 3, 3)


def sum_kernel(parts_ref, out_ref):
    total = parts_ref[0]
    for source in range(1, parts_ref.shape[0]):
        total += parts_ref[source]
    for target in range(out_ref.shape[0]):
        out_ref[target] = total


def solve_kernel(place_ref, own_ref, other_ref, prior_ref, all_ref, out_ref, work_ref):
    size = work_ref.shape[0]
    count = size // LANES
    members_dev = LANES // 4
    even = jnp.full((LANES, LANES), place_ref[1], jnp.int32) == 0
    for pairs, first, second in ((UPPER[0], own_ref, other_ref), (UPPER[1], other_ref, own_ref)):
        for position, (r, c) in enumerate(pairs):
            block = jnp.where(even, first[rows_of(position), :], second[rows_of(position), :])
            work_ref[rows_of(r), rows_of(c)] = block
            if r != c:
                work_ref[rows_of(c), rows_of(r)] = block.T
    crossed = own_ref[5 * LANES : 6 * LANES, :].T
    for r in range(count):
        work_ref[rows_of(r), size : size + members_dev] = crossed[
            :, r * members_dev : (r + 1) * members_dev
        ]
        work_ref[rows_of(r), size + members_dev :] = jnp.zeros(
            (LANES, LANES - members_dev), jnp.float32
        )
    diagonal = lax.broadcasted_iota(jnp.int32, (LANES, LANES), 0) == lax.broadcasted_iota(
        jnp.int32, (LANES, LANES), 1
    )
    unit = jnp.where(diagonal, 1.0, 0.0)
    for k in range(count):
        inverse = invert_block(work_ref[rows_of(k), rows_of(k)] + unit)
        rest = slice((k + 1) * LANES, size + LANES)
        scaled = exact_dot(inverse, work_ref[rows_of(k), rest])
        for r in range(count):
            if r != k:
                work_ref[rows_of(r), rest] -= exact_dot(work_ref[rows_of(r), rows_of(k)], scaled)
        work_ref[rows_of(k), rest] = scaled
    gain = work_ref[:, size:]
    gain = (gain - jnp.sum(gain, axis=0, keepdims=True) / size) / math.sqrt(size - 1.0)
    turned = jnp.concatenate([gain[rows_of(r)].T for r in range(count)], axis=1)[:members_dev]
    high, low = split(turned)
    both = jnp.concatenate([high, low], axis=0)
    for order in range(0, prior_ref.shape[1], 2):
        all_high, all_low = split(
            jnp.concatenate([all_ref[:, order, :], all_ref[:, order + 1, :]], axis=1)
        )
        first = jnp.dot(both, all_high, preferred_element_type=jnp.float32)
        second = jnp.dot(high, all_low, preferred_element_type=jnp.float32)
        change = first[:members_dev] + (first[members_dev:] + second)
        for side in range(2):
            out_ref[:, order + side, :] = prior_ref[:, order + side, :] + change[:, rows_of(side)]


def ring_pieces(values, gathered):
    count = lax.axis_size("member")
    turn = lambda x, step: lax.ppermute(
        x, "member", [(i, (i + 2 * step) % count) for i in range(count)]
    )
    swap = lambda x: lax.ppermute(x, "member", [(i, i ^ 1) for i in range(count)])
    below, above = [values], [values]
    for step in range(1, 5):
        below.append(turn(below[-1], 1))
        if step == 1:
            below[1], gathered = lax.optimization_barrier((below[1], gathered))
        if step < 4:
            above.append(turn(above[-1], -1))
    pieces = below[:0:-1] + above
    return pieces + [swap(piece) for piece in pieces], swap, gathered


def by_chunk(values):
    return values.reshape(-1, 2, 4, LANES).transpose(0, 2, 1, 3).reshape(-1, 8, LANES)


def by_hour(values):
    return values.reshape(-1, 4, 2, LANES).transpose(0, 2, 1, 3).reshape(-1, 2, 4 * LANES)


def shards(
    prior_params,
    lateral_flow,
    inflow_start,
    outflow_start,
    reach_count,
    downstream,
    gauge_reach,
    observed,
    obs_var,
    obs_noise,
):
    members_dev, param_count, block_dev = prior_params.shape
    members = members_dev * lax.axis_size("member")
    basins = lax.axis_size("basin")
    member_idx = lax.axis_index("member")
    place = jnp.stack([member_idx // 2, member_idx % 2]).astype(jnp.int32)
    scalars = pl.BlockSpec(memory_space=pltpu.SMEM)
    dense = pl.BlockSpec(memory_space=pltpu.VMEM)
    big = pltpu.CompilerParams(vmem_limit_bytes=40 * 2**20)
    prior_all = lax.all_gather(prior_params, "member", axis=0, tiled=True)
    outflow = predicted_outflow(
        prior_params, lateral_flow, inflow_start, outflow_start, reach_count, downstream, gauge_reach
    )
    predicted = inverse_sinh(outflow)
    pieces, swap, prior_all = ring_pieces(predicted, prior_all)
    part = pl.pallas_call(
        gram_kernel,
        in_specs=[scalars] + [dense] * 19,
        out_specs=dense,
        out_shape=jax.ShapeDtypeStruct((6 * LANES, LANES), jnp.float32),
        scratch_shapes=[
            pltpu.VMEM((members, 8 * LANES), jnp.float32),
            pltpu.VMEM((members, 8 * LANES), jnp.bfloat16),
            pltpu.VMEM((members, 8 * LANES), jnp.bfloat16),
        ],
        compiler_params=big,
    )(
        place,
        *pieces,
        by_chunk(obs_noise),
        by_chunk(observed[None])[0],
        by_chunk(obs_var[None])[0],
    )
    part = lax.all_to_all(part.reshape(basins, -1, LANES), "basin", 0, 0, tiled=True)
    summed = pl.pallas_call(
        sum_kernel, out_shape=jax.ShapeDtypeStruct(part.shape, jnp.float32), compiler_params=big
    )(part)
    own = lax.all_to_all(summed, "basin", 0, 0, tiled=True).reshape(6 * LANES, LANES)
    other = swap(own[: 5 * LANES])
    posterior = pl.pallas_call(
        solve_kernel,
        in_specs=[scalars] + [dense] * 4,
        out_specs=dense,
        out_shape=jax.ShapeDtypeStruct(prior_params.shape, jnp.float32),
        scratch_shapes=[
            pltpu.VMEM((members, members + LANES), jnp.float32),
        ],
        compiler_params=big,
    )(place, own, other, prior_params, prior_all)
    return (posterior, by_hour(predicted))


def solution(mesh):
    return jax.shard_map(
        shards,
        mesh=mesh,
        in_specs=(
            P("member", None, "basin"),
            P("member", None, "basin"),
            P("basin"),
            P("basin"),
            P("basin"),
            P("basin"),
            P("basin"),
            P(None, "basin"),
            P(None, "basin"),
            P("member", None, "basin"),
        ),
        out_specs=(P("member", None, "basin"), P("member", None, "basin")),
        check_vma=False,
    )
```

```python
import functools
import math

import jax
import jax.numpy as jnp
import numpy as np
from jax import lax
from jax.experimental import pallas as pl
from jax.experimental.pallas import tpu as pltpu
from jax.sharding import PartitionSpec as P

LANES = 128
BLK_LEV = 64
GROUP = 8
FLOW_ROWS = 256
SEND_ROWS = 272

exact_mode = lax.Precision.HIGHEST


def inverse_sinh(values):
    return jnp.log(values + jnp.sqrt(values * values + 1.0))


def two_terms(values):
    high = values.astype(jnp.bfloat16)
    low = (values - high.astype(jnp.float32)).astype(jnp.bfloat16)
    return jnp.concatenate([high, low], axis=0)


def drain_matrix(target_row):
    rows = lax.broadcasted_iota(jnp.int32, (BLK_LEV, LANES), 0).astype(jnp.float32)
    return jnp.where(rows == target_row, 1.0, 0.0).astype(jnp.bfloat16)


def drain(matrix, flows):
    return jnp.dot(matrix, two_terms(flows), preferred_element_type=jnp.float32)


def column(matrix, index):
    return jnp.broadcast_to(matrix[:, index : index + 1], (matrix.shape[0], LANES))


def wide(rows):
    return jnp.concatenate([rows[q : q + 1, :] for q in range(rows.shape[0])], axis=1)


def side_by_side(values):
    high = values.astype(jnp.bfloat16)
    return jnp.concatenate([high, (values - high.astype(jnp.float32)).astype(jnp.bfloat16)], axis=1)


def gauge_places(slot_rows):
    slots = wide(slot_rows).astype(jnp.int32)
    rows = lax.broadcasted_iota(jnp.int32, (LANES, slots.shape[1]), 0)
    picks = jnp.where(rows == (slots & 127), 1.0, 0.0).astype(jnp.bfloat16)
    return slots >> 7, jnp.concatenate([picks, picks], axis=0)


def read_gauges(flows, block_row, picks):
    picked = jnp.dot(side_by_side(flows), picks, preferred_element_type=jnp.float32)
    rows = lax.broadcasted_iota(jnp.int32, (LANES, picked.shape[1]), 0)
    mine = rows == block_row
    return [
        jnp.sum(jnp.where(mine, picked[first : first + LANES], 0.0), axis=0, keepdims=True)
        for first in range(0, flows.shape[0], LANES)
    ]


def gauge_rows(per_hour):
    return jnp.concatenate(
        [row[:, c * LANES : (c + 1) * LANES] for c in range(4) for row in per_hour], axis=0
    )


def local_kernel(
    reads, prior_ref, lateral_ref, in_ref, out_ref, down_ref, count_ref, slot_ref, modes_ref, *rest
):
    result_ref = rest[-1]
    down = jnp.broadcast_to(down_ref[...], (8, LANES)).astype(jnp.float32)
    turned = pltpu.roll(down, BLK_LEV, 1)
    left = lax.broadcasted_iota(jnp.int32, (8, LANES), 1) < BLK_LEV
    meta = jnp.concatenate(
        [
            jnp.where(left, down, turned)[:1],
            jnp.where(left, turned, down)[:1],
            count_ref[...].astype(jnp.float32),
            slot_ref[...].astype(jnp.float32),
            jnp.zeros((1, LANES), jnp.float32),
        ],
        axis=0,
    )
    storage = 0.02 + 0.1 * jax.nn.sigmoid(prior_ref[:, 0, :])
    weighting = 0.2 * jax.nn.sigmoid(prior_ref[:, 1, :])
    denominator = storage * (1.0 - weighting) + 0.5
    now = (0.5 - storage * weighting) / denominator
    back = (0.5 + storage * weighting) / denominator
    carry = 1.0 - (now + back)
    echo = back + carry * now
    counts = jnp.broadcast_to(meta[2:3, :], (GROUP, LANES))
    stacked = [now, back]
    stacked += [0.2 * prior_ref[:, 2 + order, :] for order in range(6)]
    stacked += [counts]
    stacked += [jnp.zeros((LANES - GROUP * len(stacked), LANES), jnp.float32)]
    columns = jnp.concatenate(stacked, axis=0).T
    lane_ids = lax.broadcasted_iota(jnp.int32, (LANES, LANES), 1).astype(jnp.float32)
    live = lane_ids < column(columns, 8 * GROUP)
    start_in = jnp.where(live, in_ref[...], 0.0)
    start_out = jnp.where(live, out_ref[...], 0.0)
    first_drain = drain_matrix(meta[0:1, :])
    second_drain = drain_matrix(meta[1:2, :])
    if reads:
        block_row, picks = gauge_places(meta[3:7])
    for member in range(GROUP):
        exponent = column(columns, 2 * GROUP + member) * modes_ref[0:1, :]
        for order in range(1, 6):
            exponent += column(columns, (2 + order) * GROUP + member) * modes_ref[order : order + 1, :]
        scaling = jnp.where(live, jnp.exp(exponent), 0.0)
        now_m = column(columns, member)
        back_m = column(columns, GROUP + member)
        carry_m = 1.0 - (now_m + back_m)
        side0 = lateral_ref[member, pl.ds(0, LANES, stride=2), :] * scaling
        side1 = lateral_ref[member, pl.ds(1, LANES, stride=2), :] * scaling
        steady = back_m * start_in + carry_m * start_out
        passed = None
        flows = []
        for level, matrix in ((0, first_drain), (1, second_drain)):
            part = slice(level * BLK_LEV, (level + 1) * BLK_LEV)
            inflow0, inflow1 = side0[part], side1[part]
            if passed is not None:
                inflow0 += jnp.where(live[part], passed[:, :LANES], 0.0)
                inflow1 += jnp.where(live[part], passed[:, LANES:], 0.0)
            outflow0 = now_m[part] * inflow0 + steady[part]
            outflow1 = now_m[part] * inflow1 + back_m[part] * inflow0 + carry_m[part] * outflow0
            if level == 0 or not reads:
                passed = drain(matrix, jnp.concatenate([outflow0, outflow1], axis=1))
            flows.append((outflow0, outflow1))
        if reads:
            whole = jnp.concatenate([flows[level][hour] for hour in range(2) for level in range(2)], axis=0)
            result_ref[member] = gauge_rows(read_gauges(whole, block_row, picks))
            continue
        for hour in range(2):
            first_row = ((member % 2) * 2 + hour) * BLK_LEV
            result_ref[member // 2, first_row : first_row + BLK_LEV, :] = passed[
                :, hour * LANES : (hour + 1) * LANES
            ]
    if reads:
        return
    for pair in range(GROUP // 2):
        result_ref[pair, FLOW_ROWS : FLOW_ROWS + 8, :] = jnp.concatenate(
            [
                now[2 * pair : 2 * pair + 2],
                echo[2 * pair : 2 * pair + 2],
                meta[2:3],
                jnp.zeros((3, LANES), jnp.float32),
            ],
            axis=0,
        )
        result_ref[pair, FLOW_ROWS + 8 : FLOW_ROWS + 16, :] = meta


def cascade_kernel(got_ref, _, out_ref):
    sources = got_ref.shape[0]
    coefs = [got_ref[source, FLOW_ROWS : FLOW_ROWS + 8, :] for source in range(sources)]
    columns = jnp.concatenate(coefs, axis=0).T
    lane_ids = lax.broadcasted_iota(jnp.int32, (LANES, LANES), 1).astype(jnp.float32)

    def flow(source):
        parts = [
            got_ref[source, (member * 2 + hour) * BLK_LEV : (member * 2 + hour + 1) * BLK_LEV, :]
            for hour in range(2)
            for member in range(2)
        ]
        return jnp.concatenate(parts, axis=1)

    out_ref[0] = jnp.zeros(out_ref.shape[1:], jnp.float32)
    upstream = flow(0)
    for source in range(1, sources):
        meta = got_ref[source, FLOW_ROWS + 8 : FLOW_ROWS + 16, :]
        live = lane_ids < column(columns, 8 * source + 4)
        now = [jnp.where(live, column(columns, 8 * source + member), 0.0) for member in range(2)]
        echo = [jnp.where(live, column(columns, 8 * source + 2 + member), 0.0) for member in range(2)]
        routed = []
        for level in range(2):
            part = slice(level * BLK_LEV, (level + 1) * BLK_LEV)
            first = [now[m][part] * upstream[:, m * LANES : (m + 1) * LANES] for m in range(2)]
            second = [
                now[m][part] * upstream[:, (2 + m) * LANES : (3 + m) * LANES]
                + echo[m][part] * upstream[:, m * LANES : (m + 1) * LANES]
                for m in range(2)
            ]
            routed.append(first + second)
            if level == 0 or source < sources - 1:
                upstream = drain(
                    drain_matrix(meta[level : level + 1, :]), jnp.concatenate(first + second, axis=1)
                )
        if source < sources - 1:
            upstream += flow(source)
        block_row, picks = gauge_places(meta[3:7])
        whole = jnp.concatenate(
            [
                routed[level][hour * 2 + member]
                for member in range(2)
                for hour in range(2)
                for level in range(2)
            ],
            axis=0,
        )
        read = read_gauges(whole, block_row, picks)
        out_ref[source] = jnp.concatenate([gauge_rows(read[:2]), gauge_rows(read[2:])], axis=0)


def predicted_outflow(
    prior_params, lateral_flow, inflow_start, outflow_start, reach_count, downstream, gauge_reach
):
    members_dev, param_count, block_dev = prior_params.shape
    basins = lax.axis_size("basin")
    orders = np.arange(8)[:, None]
    modes = np.cos(math.pi * orders * (np.arange(LANES)[None, :] + 0.5) / LANES).astype(np.float32)
    lateral_rows = (
        lateral_flow.reshape(members_dev, 2, block_dev, LANES)
        .transpose(0, 2, 1, 3)
        .reshape(members_dev, 2 * block_dev, LANES)
    )
    whole = lambda step: (0, 0)
    operands = (
        prior_params,
        lateral_rows,
        inflow_start.reshape(block_dev, LANES),
        outflow_start.reshape(block_dev, LANES),
        downstream.reshape(1, block_dev),
        reach_count.reshape(1, block_dev),
        gauge_reach.reshape(4, LANES),
        jnp.asarray(modes),
    )
    blocks = [
        pl.BlockSpec((GROUP, param_count, LANES), lambda step: (step, 0, 0)),
        pl.BlockSpec((GROUP, 2 * block_dev, LANES), lambda step: (step, 0, 0)),
        pl.BlockSpec((block_dev, LANES), whole),
        pl.BlockSpec((block_dev, LANES), whole),
        pl.BlockSpec((1, LANES), whole),
        pl.BlockSpec((1, LANES), whole),
        pl.BlockSpec((4, LANES), whole),
        pl.BlockSpec((8, LANES), whole),
    ]
    roomy = pltpu.CompilerParams(vmem_limit_bytes=60 * 2**20)
    sent = pl.pallas_call(
        functools.partial(local_kernel, False),
        grid=(members_dev // GROUP,),
        in_specs=blocks,
        out_specs=pl.BlockSpec((GROUP // 2, SEND_ROWS, LANES), lambda step: (step, 0, 0)),
        out_shape=jax.ShapeDtypeStruct((members_dev // 2, SEND_ROWS, LANES), jnp.float32),
        compiler_params=roomy,
    )(*operands)
    local = pl.pallas_call(
        functools.partial(local_kernel, True),
        grid=(members_dev // GROUP,),
        in_specs=blocks + [pl.BlockSpec((1, 8, LANES), lambda step: (0, 0, 0))],
        out_specs=pl.BlockSpec((GROUP, 8, LANES), lambda step: (step, 0, 0)),
        out_shape=jax.ShapeDtypeStruct((members_dev, 8, LANES), jnp.float32),
        compiler_params=roomy,
    )(*operands, sent)
    got = lax.all_to_all(sent, "basin", 0, 0, tiled=True)
    extra = pl.pallas_call(
        cascade_kernel,
        in_specs=[pl.BlockSpec(memory_space=pltpu.VMEM), pl.BlockSpec(memory_space=pltpu.HBM)],
        out_shape=jax.ShapeDtypeStruct((basins, 16, LANES), jnp.float32),
        compiler_params=pltpu.CompilerParams(vmem_limit_bytes=40 * 2**20),
    )(got, local)
    extra = lax.all_to_all(extra, "basin", 0, 0, tiled=True)
    return local + extra.reshape(members_dev, 8, LANES)


def full(row, lane):
    return jnp.broadcast_to(row[:, lane : lane + 1], (8, LANES))

def product(a, b):
    return [
        [sum_terms([a[i][k] * b[k][j] for k in range(len(b))]) for j in range(len(b[0]))]
        for i in range(len(a))
    ]


def sum_terms(terms):
    while len(terms) > 1:
        terms = [terms[i] + terms[i + 1] for i in range(0, len(terms), 2)]
    return terms[0]


def flipped(a):
    return [list(row) for row in zip(*a)]


def symmetric_inverse(p):
    half = len(p) // 2
    if len(p) == 2:
        scale = 1.0 / (p[0][0] * p[1][1] - p[0][1] * p[0][1])
        cross = -p[0][1] * scale
        return [[p[1][1] * scale, cross], [cross, p[0][0] * scale]]
    corner = [row[half:] for row in p[:half]]
    first = symmetric_inverse([row[:half] for row in p[:half]])
    lifted = product(first, corner)
    shift = product(flipped(corner), lifted)
    second = symmetric_inverse(
        [[p[half + i][half + j] - shift[i][j] for j in range(half)] for i in range(half)]
    )
    moved = product(lifted, second)
    back = product(moved, flipped(lifted))
    top = [
        [first[i][j] + back[i][j] for j in range(half)] + [-moved[i][j] for j in range(half)]
        for i in range(half)
    ]
    low = [[-moved[j][i] for j in range(half)] + second[i] for i in range(half)]
    return top + low


PIVOT = 8


def invert_block(block):
    tiles = [block[8 * t : 8 * t + 8, :] for t in range(16)]
    lanes = lax.broadcasted_iota(jnp.int32, (8, LANES), 1)
    subs = lax.broadcasted_iota(jnp.int32, (8, LANES), 0)
    for first in range(0, LANES, PIVOT):
        home, offset = first // 8, first % 8
        rows = [
            jnp.broadcast_to(tiles[home][offset + i : offset + i + 1, :], (8, LANES))
            for i in range(PIVOT)
        ]
        pivots = [
            [full(rows[min(i, j)], first + max(i, j)) if i <= j else None for j in range(PIVOT)]
            for i in range(PIVOT)
        ]
        pivots = [[pivots[min(i, j)][max(i, j)] for j in range(PIVOT)] for i in range(PIVOT)]
        inverse = symmetric_inverse(pivots)
        group = (lanes >= first) & (lanes < first + PIVOT)
        units = [
            jnp.where(group, jnp.where(lanes == first + i, 1.0, 0.0), rows[i]) for i in range(PIVOT)
        ]
        fresh = [sum_terms([inverse[i][j] * units[j] for j in range(PIVOT)]) for i in range(PIVOT)]
        for t in range(16):
            cols = [full(tiles[t], first + i) for i in range(PIVOT)]
            updated = jnp.where(group, 0.0, tiles[t]) - sum_terms(
                [cols[i] * fresh[i] for i in range(PIVOT)]
            )
            if t == home:
                for i in range(PIVOT):
                    updated = jnp.where(subs == offset + i, fresh[i], updated)
            tiles[t] = updated
    return jnp.concatenate(tiles, axis=0)


def exact_dot(a, b):
    return jnp.dot(a, b, precision=exact_mode, preferred_element_type=jnp.float32)


UPPER = (((0, 0), (0, 1), (0, 2), (0, 3), (1, 1)), ((1, 2), (1, 3), (2, 2), (2, 3), (3, 3)))


def rows_of(index):
    return slice(index * LANES, (index + 1) * LANES)


def split(values):
    high = values.astype(jnp.bfloat16)
    return high, (values - high.astype(jnp.float32)).astype(jnp.bfloat16)


def pair_dot(left, right):
    rows = left[0].shape[0]
    stacked = jnp.concatenate(left, axis=0)
    high, low = [
        lax.dot_general(
            stacked, part, (((1,), (1,)), ((), ())), preferred_element_type=jnp.float32
        )
        for part in right
    ]
    return high[:rows] + (high[rows:] + low[:rows]) + low[rows:]


def gram_kernel(place_ref, *refs):
    pieces, (noise_ref, observed_ref, var_ref, out_ref, rows_ref, high_ref, low_ref) = (
        refs[:16],
        refs[16:],
    )
    zone, core = place_ref[0], place_ref[1]
    members_dev = noise_ref.shape[0]
    members, width = rows_ref.shape
    for piece, ref in enumerate(pieces):
        ring = piece % 8
        owner = lax.rem(zone + ring + 4, 8) * 2 + (core if piece < 8 else 1 - core)
        first = pl.multiple_of(owner * members_dev, members_dev)
        for q in range(8):
            rows_ref[pl.ds(first, members_dev), q * LANES : (q + 1) * LANES] = ref[:, q, :]
    spread = 2.0 * jnp.sqrt(wide(var_ref[...]))
    mean = jnp.sum(rows_ref[...], axis=0, keepdims=True) / members
    own = jnp.concatenate([pieces[4][:, q, :] for q in range(8)], axis=1)
    noise = jnp.concatenate([noise_ref[:, q, :] for q in range(8)], axis=1)
    innovation = (wide(observed_ref[...]) + spread * noise - own) / spread
    scale = 1.0 / (math.sqrt(members - 1.0) * spread)
    high_ref[...], low_ref[...] = split((rows_ref[...] - mean) * scale)
    crossed = pair_dot(split(innovation), (high_ref[...], low_ref[...]))
    for c in range(4):
        first = 5 * LANES + c * members_dev
        out_ref[first : first + members_dev, :] = crossed[:, rows_of(c)]

    def fill(position, row, first_col, last_col):
        columns = slice(first_col * LANES, (last_col + 1) * LANES)
        product = pair_dot(
            (high_ref[rows_of(row), :], low_ref[rows_of(row), :]),
            (high_ref[columns, :], low_ref[columns, :]),
        )
        for c in range(last_col - first_col + 1):
            out_ref[rows_of(position + c), :] = product[:, rows_of(c)]

    @pl.when(core == 0)
    def _():
        fill(0, 0, 0, 3)
        fill(4, 1, 1, 1)

    @pl.when(core == 1)
    def _():
        fill(0, 1, 2, 3)
        fill(2, 2, 2, 3)
        fill(4, 3, 3, 3)


def sum_kernel(parts_ref, out_ref):
    total = parts_ref[0]
    for source in range(1, parts_ref.shape[0]):
        total += parts_ref[source]
    for target in range(out_ref.shape[0]):
        out_ref[target] = total


def solve_kernel(place_ref, own_ref, other_ref, prior_ref, all_ref, out_ref, work_ref):
    size = work_ref.shape[0]
    count = size // LANES
    members_dev = LANES // 4
    even = jnp.full((LANES, LANES), place_ref[1], jnp.int32) == 0
    for pairs, first, second in ((UPPER[0], own_ref, other_ref), (UPPER[1], other_ref, own_ref)):
        for position, (r, c) in enumerate(pairs):
            block = jnp.where(even, first[rows_of(position), :], second[rows_of(position), :])
            work_ref[rows_of(r), rows_of(c)] = block
            if r != c:
                work_ref[rows_of(c), rows_of(r)] = block.T
    crossed = own_ref[5 * LANES : 6 * LANES, :].T
    for r in range(count):
        work_ref[rows_of(r), size : size + members_dev] = crossed[
            :, r * members_dev : (r + 1) * members_dev
        ]
        work_ref[rows_of(r), size + members_dev :] = jnp.zeros(
            (LANES, LANES - members_dev), jnp.float32
        )
    diagonal = lax.broadcasted_iota(jnp.int32, (LANES, LANES), 0) == lax.broadcasted_iota(
        jnp.int32, (LANES, LANES), 1
    )
    unit = jnp.where(diagonal, 1.0, 0.0)
    for k in range(count):
        inverse = invert_block(work_ref[rows_of(k), rows_of(k)] + unit)
        rest = slice((k + 1) * LANES, size + LANES)
        scaled = exact_dot(inverse, work_ref[rows_of(k), rest])
        for r in range(count):
            if r != k:
                work_ref[rows_of(r), rest] -= exact_dot(work_ref[rows_of(r), rows_of(k)], scaled)
        work_ref[rows_of(k), rest] = scaled
    gain = work_ref[:, size:]
    gain = (gain - jnp.sum(gain, axis=0, keepdims=True) / size) / math.sqrt(size - 1.0)
    turned = jnp.concatenate([gain[rows_of(r)].T for r in range(count)], axis=1)[:members_dev]
    high, low = split(turned)
    both = jnp.concatenate([high, low], axis=0)
    for order in range(0, prior_ref.shape[1], 4):
        all_high, all_low = split(
            jnp.concatenate([all_ref[:, order + side, :] for side in range(4)], axis=1)
        )
        first = jnp.dot(both, all_high, preferred_element_type=jnp.float32)
        second = jnp.dot(high, all_low, preferred_element_type=jnp.float32)
        change = first[:members_dev] + (first[members_dev:] + second)
        for side in range(4):
            out_ref[:, order + side, :] = prior_ref[:, order + side, :] + change[:, rows_of(side)]


def ring_pieces(values, gathered):
    count = lax.axis_size("member")
    turn = lambda x, step: lax.ppermute(
        x, "member", [(i, (i + 2 * step) % count) for i in range(count)]
    )
    swap = lambda x: lax.ppermute(x, "member", [(i, i ^ 1) for i in range(count)])
    below, above = [values], [values]
    for step in range(1, 5):
        below.append(turn(below[-1], 1))
        if step == 1:
            below[1], gathered = lax.optimization_barrier((below[1], gathered))
        if step < 4:
            above.append(turn(above[-1], -1))
    pieces = below[:0:-1] + above
    return pieces + [swap(piece) for piece in pieces], swap, gathered


def by_chunk(values):
    return values.reshape(-1, 2, 4, LANES).transpose(0, 2, 1, 3).reshape(-1, 8, LANES)


def by_hour(values):
    return values.reshape(-1, 4, 2, LANES).transpose(0, 2, 1, 3).reshape(-1, 2, 4 * LANES)


def shards(
    prior_params,
    lateral_flow,
    inflow_start,
    outflow_start,
    reach_count,
    downstream,
    gauge_reach,
    observed,
    obs_var,
    obs_noise,
):
    members_dev, param_count, block_dev = prior_params.shape
    members = members_dev * lax.axis_size("member")
    basins = lax.axis_size("basin")
    member_idx = lax.axis_index("member")
    place = jnp.stack([member_idx // 2, member_idx % 2]).astype(jnp.int32)
    scalars = pl.BlockSpec(memory_space=pltpu.SMEM)
    dense = pl.BlockSpec(memory_space=pltpu.VMEM)
    big = pltpu.CompilerParams(vmem_limit_bytes=40 * 2**20)
    prior_all = lax.all_gather(prior_params, "member", axis=0, tiled=True)
    outflow = predicted_outflow(
        prior_params, lateral_flow, inflow_start, outflow_start, reach_count, downstream, gauge_reach
    )
    predicted = inverse_sinh(outflow)
    pieces, swap, prior_all = ring_pieces(predicted, prior_all)
    part = pl.pallas_call(
        gram_kernel,
        in_specs=[scalars] + [dense] * 19,
        out_specs=dense,
        out_shape=jax.ShapeDtypeStruct((6 * LANES, LANES), jnp.float32),
        scratch_shapes=[
            pltpu.VMEM((members, 8 * LANES), jnp.float32),
            pltpu.VMEM((members, 8 * LANES), jnp.bfloat16),
            pltpu.VMEM((members, 8 * LANES), jnp.bfloat16),
        ],
        compiler_params=big,
    )(
        place,
        *pieces,
        by_chunk(obs_noise),
        by_chunk(observed[None])[0],
        by_chunk(obs_var[None])[0],
    )
    part = lax.all_to_all(part.reshape(basins, -1, LANES), "basin", 0, 0, tiled=True)
    summed = pl.pallas_call(
        sum_kernel, out_shape=jax.ShapeDtypeStruct(part.shape, jnp.float32), compiler_params=big
    )(part)
    own = lax.all_to_all(summed, "basin", 0, 0, tiled=True).reshape(6 * LANES, LANES)
    other = swap(own[: 5 * LANES])
    posterior = pl.pallas_call(
        solve_kernel,
        in_specs=[scalars] + [dense] * 4,
        out_specs=dense,
        out_shape=jax.ShapeDtypeStruct(prior_params.shape, jnp.float32),
        scratch_shapes=[
            pltpu.VMEM((members, members + LANES), jnp.float32),
        ],
        compiler_params=big,
    )(place, own, other, prior_params, prior_all)
    return (posterior, by_hour(predicted))


def solution(mesh):
    return jax.shard_map(
        shards,
        mesh=mesh,
        in_specs=(
            P("member", None, "basin"),
            P("member", None, "basin"),
            P("basin"),
            P("basin"),
            P("basin"),
            P("basin"),
            P("basin"),
            P(None, "basin"),
            P(None, "basin"),
            P("member", None, "basin"),
        ),
        out_specs=(P("member", None, "basin"), P("member", None, "basin")),
        check_vma=False,
    )
```
